32 devices in a mesh: band: 2 (over y), col: 4 (over z), row: 2 (over x), vis: 2 (over core).
Axes of the slice: x: 2, y: 2, z: 4, core: 2. Of those that a mesh axis runs over, the one named last changes fastest.
Arguments:
- visibilities: bfloat16 [3072, 2, 256], P(('band', 'col', 'row', 'vis')), parts along dimension 0, may hold values from -6 to 6
- coords: float32 [3072, 2, 256], P(('band', 'col', 'row', 'vis')), parts along dimension 0, may hold values from -0.5 to 0.5
- block_subgrid: int32 [3072], P(('band', 'col', 'row', 'vis')), parts along dimension 0, may hold values from 0 to 1023, as said below
- baseline_ids: int32 [3072], P(('band', 'col', 'row', 'vis')), parts along dimension 0, may hold values from 0 to 130815
- live_blocks: int32 [32], P(('band', 'col', 'row', 'vis')), parts along dimension 0, may hold values from 48 to 96, as said below
- subgrid_place: int32 [3, 2048], P(None, ('band', 'col', 'row', 'vis')), parts along dimension 1, may hold values from 0 to 1984, as said below
- baseline_weight: float32 [130816], replicated, may hold values from 0.2 to 2
- tapering: float32 [64, 64], replicated, may hold values from 0.2 to 1
- plane_phase: float32 [8, 64, 64], replicated, may hold values from -3.140625 to 3.140625
Outputs:
- grid: float32 [2, 4096, 1024], P(None, ('band', 'col'), ('row', 'vis')), parts along dimension 1
The draws below stay inside these ranges and needn't reach their ends.
There are 2 independent parts, one for each index of `band`. The reference program is written for one: setup_inputs(seed, part) draws one part's arguments, and reference() takes and returns one part's arrays. A program takes and returns all parts, laid end to end along the dimension named above; an argument that names none is the same for every part. Nothing has to cross between parts.
Inputs may be any that keep to these rules, and one draw needn't show every extreme that they name: `block_subgrid`: subgrid s is owned by the device s // 64, devices counted in the order col, row, vis. Of the 96 blocks of one device at most 24 name subgrids of one owner, and in every draw some owner is named 24 times by the blocks of every device. `live_blocks`: blocks j of device d with j >= entry d carry no weight. Some device has all 96 blocks live and some has 48. `subgrid_place`: row 2 is a subgrid's w-plane, below 8. Every subgrid lies inside one facet: for some c and r its u cells lie in c * 512 .. (c + 1) * 512 - 1 and its v cells in r * 512 .. (r + 1) * 512 - 1. At most 16 of one owner's 64 subgrids lie in one facet, and in every draw the last facet holds 16 subgrids of every owner.
All inputs are finite; a program needn't handle non-finite values.
Results may differ from the reference program's by a relative error of at most 0.0037.
Values sent between devices are 32-bit elements; how exact they have to be, the bound alone decides.
A program may use at most 128 MiB of HBM per device.

```python
import math
import jax
import jax.numpy as jnp
from jax import lax

SG = 64
BV = 256
NW = 8
NBASE = 130816
NBLK = 96
SUB_DEV = 64
FU = 512
FV = 512
NDEV = 16
FACETS = 8
OWNER_BLOCK_LIMIT = 24
SCAP = 16
SLOT_COUNT = 384
NBLOCKS = 1536
NU = 2048
NV = 1024


def draw_block_subgrid(key, part):
    key = jax.random.fold_in(key, 11)
    key_appeal, key_top, key_rest = jax.random.split(key, 3)
    favourite = jax.random.randint(key_top, (), 0, NDEV)
    owner_preference = jax.random.randint(key_appeal, (NDEV,), 0, 4)
    owner_ids = jnp.arange(NDEV)
    owner_preference = jnp.where((owner_ids == favourite) | (owner_ids == 0) | (owner_ids == NDEV - 1), 8, owner_preference)
    owner_of_slot = jnp.arange(SLOT_COUNT) // OWNER_BLOCK_LIMIT

    def one_device(device_key):
        noise_random_key, key_order, key_local = jax.random.split(device_key, 3)
        random_jitter = jax.random.randint(noise_random_key, (SLOT_COUNT,), 0, 2 ** 18)
        placement_score = (random_jitter + owner_preference[owner_of_slot] * 2 ** 16) * SLOT_COUNT + jnp.arange(SLOT_COUNT)
        _, picked = lax.top_k(placement_score, NBLK)
        owners = owner_of_slot[picked]
        local = jax.random.randint(key_local, (NBLK,), 0, SUB_DEV)
        index = jnp.arange(NBLK)
        first_low = jnp.argmax((owners == 0).astype(jnp.int32))
        first_high = jnp.argmax((owners == NDEV - 1).astype(jnp.int32))
        local = jnp.where(index == first_low, 0, local)
        local = jnp.where(index == first_high, SUB_DEV - 1, local)
        order = jax.random.permutation(key_order, NBLK)
        return owners[order] * SUB_DEV + local[order]
    keys = jax.random.split(key_rest, NDEV)
    return jax.vmap(one_device)(keys).reshape(NDEV * NBLK).astype(jnp.int32)


def draw_live_blocks(key, part):
    key = jax.random.fold_in(key, 23)
    key_count, key_full = jax.random.split(key)
    counts = jax.random.randint(key_count, (NDEV,), NBLK // 2, NBLK + 1)
    fullest = jax.random.randint(key_full, (), 0, NDEV)
    device = jnp.arange(NDEV)
    counts = jnp.where(device == fullest, NBLK, counts)
    counts = jnp.where(device == (fullest + 1) % NDEV, NBLK // 2, counts)
    return counts.astype(jnp.int32)


def draw_subgrid_place(key, part):
    key = jax.random.fold_in(key, 37)
    key_rest = jax.random.fold_in(key, 1)
    crowded = FACETS - 1
    facet_rows = NV // FV

    def one_owner(owner_key):
        key_slots, key_order, key_u, key_v, key_plane = jax.random.split(owner_key, 5)
        others = jax.random.permutation(key_slots, (FACETS - 1) * SCAP)[:SUB_DEV - SCAP] // SCAP
        facet = jnp.concatenate([jnp.full((SCAP,), crowded, jnp.int32), others.astype(jnp.int32)])
        offset_u = jax.random.randint(key_u, (SUB_DEV,), 0, FU - SG + 1)
        offset_v = jax.random.randint(key_v, (SUB_DEV,), 0, FV - SG + 1)
        plane = jax.random.randint(key_plane, (SUB_DEV,), 0, NW)
        first = jnp.arange(SUB_DEV) == 0
        offset_u = jnp.where(first, FU - SG, offset_u)
        offset_v = jnp.where(first, FV - SG, offset_v)
        plane = jnp.where(first, 0, plane)
        order = jax.random.permutation(key_order, SUB_DEV)
        facet = facet[order]
        offset_u = offset_u[order]
        offset_v = offset_v[order]
        plane = plane[order]
        return jnp.stack([facet // facet_rows * FU + offset_u, facet % facet_rows * FV + offset_v, plane])
    keys = jax.random.split(key_rest, NDEV)
    placed = jax.vmap(one_owner)(keys)
    return jnp.transpose(placed, (1, 0, 2)).reshape(3, NDEV * SUB_DEV).astype(jnp.int32)


def place_ends(array, own_key, smallest, top_value):
    longest = array.shape.index(max(array.shape))
    spots = []
    for shift in (0, 1):
        where = [jax.random.randint(jax.random.fold_in(own_key, axis), (), 0, length) for axis, length in enumerate(array.shape)]
        where[longest] = (where[longest] + shift) % array.shape[longest]
        spots.append(tuple(where))
    return array.at[spots[0]].set(smallest).at[spots[1]].set(top_value)


def level_of(rng, extent, shards, low, largest):
    def one(dim, blocks):
        draws = jax.random.uniform(jax.random.fold_in(jax.random.fold_in(rng, 6), dim), (blocks,), jnp.float32, low / len(shards), largest / len(shards))
        return jnp.repeat(jnp.exp(draws), extent[dim] // blocks).reshape((-1,) + (1,) * (len(extent) - dim - 1))

    factor_of = one(*shards[0])
    for cut in shards[1:]:
        factor_of = factor_of * one(*cut)
    return factor_of


def gaussian(own_key, dims, scale, most, cuts=(), held_as=jnp.bfloat16):
    level = level_of(own_key, dims, cuts, -0.22, 0.18) if cuts else 1.0
    array = jax.random.normal(own_key, dims, jnp.float32) * scale * level
    return jnp.minimum(jnp.maximum(array, -most), most).astype(held_as)


def setup_inputs(seed: int = 0, part: int = 0) -> dict:
    splits = jax.random.split(jax.random.key(seed), 10)
    part_keys = jax.random.split(jax.random.fold_in(splits[9], part), 10)
    return {
        "visibilities": gaussian(part_keys[0], (NBLOCKS, 2, BV), 1.0, 6.0, ((0, 16),)),
        "coords": jnp.clip(jax.random.uniform(part_keys[1], (NBLOCKS, 2, BV), jnp.float32, -0.5, 0.5) * level_of(part_keys[1], (NBLOCKS, 2, BV), ((0, 16),), -0.4, 0.0), -0.5, 0.5),
        "block_subgrid": draw_block_subgrid(jax.random.fold_in(jax.random.fold_in(splits[9], part), 71), part),
        "baseline_ids": place_ends(jax.random.randint(part_keys[3], (NBLOCKS,), 0, NBASE), jax.random.fold_in(part_keys[3], 1), 0, NBASE - 1).astype(jnp.int32),
        "live_blocks": draw_live_blocks(jax.random.fold_in(jax.random.fold_in(splits[9], part), 71), part),
        "subgrid_place": draw_subgrid_place(jax.random.fold_in(jax.random.fold_in(splits[9], part), 71), part),
        "baseline_weight": jnp.clip(jnp.exp(jax.random.uniform(splits[6], (NBASE,), jnp.float32, math.log(0.2), math.log(2.0))), 0.2, 2.0),
        "tapering": jnp.clip(jnp.exp(jax.random.uniform(splits[7], (SG, SG), jnp.float32, math.log(0.2), math.log(1.0))), 0.2, 1.0),
        "plane_phase": jnp.clip(jax.random.uniform(splits[8], (NW, SG, SG), jnp.float32, -3.140625, 3.140625), -3.140625, 3.140625),
    }


def kernel_operands(coords, weighted):
    centred = (jnp.arange(SG) - SG // 2).astype(coords.dtype)
    angle_u = 2.0 * math.pi * coords[:, 0, :, None] * centred
    vertical_angle = 2.0 * math.pi * coords[:, 1, :, None] * centred
    kern_ure = jnp.cos(angle_u)
    kern_uim = jnp.sin(angle_u)
    kernel_vertical_real = jnp.cos(vertical_angle)
    kernel_vertical_imag = jnp.sin(vertical_angle)
    vis_real = weighted[:, 0, :, None]
    vis_imag = weighted[:, 1, :, None]
    scaled_re = vis_real * kern_ure - vis_imag * kern_uim
    scaled_im = vis_real * kern_uim + vis_imag * kern_ure
    left_side = jnp.concatenate([scaled_re, scaled_im], axis=1).astype(jnp.bfloat16)
    upper_limit = jnp.concatenate([kernel_vertical_real, kernel_vertical_imag], axis=2)
    lower_limit = jnp.concatenate([-kernel_vertical_imag, kernel_vertical_real], axis=2)
    right_side = jnp.concatenate([upper_limit, lower_limit], axis=1).astype(jnp.bfloat16)
    return (left_side, right_side)

def reference(visibilities, coords, block_subgrid, baseline_ids, live_blocks, subgrid_place, baseline_weight, tapering, plane_phase):
    total = visibilities.shape[0]
    position = jnp.arange(total, dtype=jnp.int32)
    live = position % NBLK < live_blocks[position // NBLK]
    weight = jnp.where(live, baseline_weight[baseline_ids], jnp.zeros((), baseline_weight.dtype))
    weighted = visibilities.astype(jnp.float32) * weight[:, None, None]
    group = math.gcd(total, 256)
    steps = total // group
    nsub = subgrid_place.shape[1]

    def grid_group(subgrid_sum, items):
        part_vis, part_coords, part_sub = items
        left_side, right_side = kernel_operands(part_coords, part_vis)
        image = jnp.einsum('gkx,gky->gxy', left_side.astype(jnp.float32), right_side.astype(jnp.float32), precision=lax.Precision.HIGHEST)
        return (subgrid_sum.at[part_sub].add(image), None)
    start = jnp.zeros((nsub, SG, 2 * SG), jnp.float32)
    subgrid_sum, _ = lax.scan(grid_group, start, (weighted.reshape(steps, group, 2, BV), coords.reshape(steps, group, 2, BV), block_subgrid.reshape(steps, group)))
    image_re = subgrid_sum[:, :, :SG]
    image_im = subgrid_sum[:, :, SG:]
    phase = plane_phase[subgrid_place[2]]
    screen_re = tapering * jnp.cos(phase)
    screen_im = tapering * jnp.sin(phase)
    masked_re = image_re * screen_re - image_im * screen_im
    masked_im = image_re * screen_im + image_im * screen_re
    spectrum = jnp.fft.fft2(masked_re + 1j * masked_im) / (SG * math.sqrt(BV))
    pieces = jnp.stack([spectrum.real, spectrum.imag], axis=1).astype(subgrid_sum.dtype)

    def place_one(item, whole):
        corner_u = subgrid_place[0, item]
        corner_v = subgrid_place[1, item]
        anchor = jnp.zeros((), jnp.int32)
        before = lax.dynamic_slice(whole, (anchor, corner_u, corner_v), (2, SG, SG))
        return lax.dynamic_update_slice(whole, before + pieces[item], (anchor, corner_u, corner_v))
    return lax.fori_loop(0, nsub, place_one, jnp.zeros((2, NU, NV), subgrid_sum.dtype))
```

```python
import functools
import math

import jax
import jax.numpy as jnp
import numpy as np
from jax import lax
from jax.experimental import pallas as pl
from jax.experimental.pallas import tpu as pltpu
from jax.sharding import PartitionSpec as P

SG = 64
BV = 256
FU = 512
FV = 512
LANES = 128
TILES = FV // LANES
UNROLL = 4
FFT_UNROLL = 4
BIG = 1 << 30


def _poly(fn, terms):
    y = np.cos(np.pi * (np.arange(400) + 0.5) / 400)
    s = 0.25 * 0.5 * (y + 1.0)
    fit = np.polynomial.chebyshev.Chebyshev.fit(s, fn(np.sqrt(s)), terms - 1, domain=[0.0, 0.25])
    return [float(c) for c in fit.convert(kind=np.polynomial.Polynomial, domain=[-1, 1]).coef]


COS_COEF = _poly(lambda t: np.cos(2 * np.pi * t), 8)
SIN_COEF = _poly(lambda t: np.sin(2 * np.pi * t) / t, 7)


def _horner(coef, s):
    out = jnp.full_like(s, coef[-1])
    for c in coef[-2::-1]:
        out = out * s + c
    return out


def _fine(turns, steps):
    t = turns * steps
    t = t - jnp.round(t)
    s = t * t
    return _horner(COS_COEF, s), t * _horner(SIN_COEF, s)


def _powers(turns, steps, scale):
    er, ei = _fine(turns, steps)
    z4r = jnp.broadcast_to(er[4:5], er.shape)
    z4i = jnp.broadcast_to(ei[4:5], ei.shape)

    def square(r, i):
        return r * r - i * i, 2.0 * (r * i)

    z1 = square(z4r, z4i)
    z2 = square(*z1)
    z3 = (z1[0] * z2[0] - z1[1] * z2[1], z1[0] * z2[1] + z1[1] * z2[0])
    z4 = square(*z2)
    if scale is not None:
        wr, wi = scale
        er, ei = er * wr - ei * wi, er * wi + ei * wr
    real = [None] * 8
    imag = [None] * 8
    real[4], imag[4] = er, ei
    for a, (zr, zi) in ((1, z1), (2, z2), (3, z3), (4, z4)):
        rr, ii, ri, ir = er * zr, ei * zi, er * zi, ei * zr
        real[4 - a], imag[4 - a] = rr + ii, ir - ri
        if a < 4:
            real[4 + a], imag[4 + a] = rr - ii, ri + ir
    return jnp.concatenate(real + imag, axis=0).astype(jnp.bfloat16)


def _block_product(block_ref, index, steps):
    left, right = [], []
    for h in range(2):
        def row(k):
            return jnp.broadcast_to(block_ref[index, 2 * k + h : 2 * k + h + 1, :], (8, LANES))

        left.append(_powers(row(2), steps, (row(0), row(1))))
        right.append(_powers(row(3), steps, None))
    return lax.dot_general(
        jnp.concatenate(left, axis=1),
        jnp.concatenate(right, axis=1),
        (((1,), (1,)), ((), ())),
        preferred_element_type=jnp.float32,
    )


def _split(x):
    hi = x.astype(jnp.bfloat16)
    lo = (x - hi.astype(jnp.float32)).astype(jnp.bfloat16)
    return hi, lo


def _combine(four, sign):
    return four[:SG] + pltpu.roll(four[SG:], SG, 1) * sign


def facet_kernel(
    shift,
    subs,
    count_ref,
    keys_ref,
    place_ref,
    vis_ref,
    block_ref,
    screen_a_ref,
    screen_b_ref,
    right_ref,
    left_ref,
    mine_ref,
    theirs_ref,
    sums,
    facet,
    found,
):
    trash = sums.shape[0] - 1
    steps = lax.broadcasted_iota(jnp.int32, (8, LANES), 0).astype(jnp.float32)
    lane = lax.broadcasted_iota(jnp.int32, (SG, LANES), 1)
    sign = jnp.where(lane < SG, -1.0, 1.0)
    facet[...] = jnp.zeros_like(facet)
    count = count_ref[0]

    def grid_blocks(step, carry):
        last_sub, slot = carry
        jobs = []
        for k in range(UNROLL):
            at = step * UNROLL + k
            key = keys_ref[at]
            real = at < count
            index = jnp.where(real, key & ((1 << shift) - 1), 0)
            sub = jnp.where(real, key >> shift, last_sub)
            fresh = sub != last_sub
            slot = slot + fresh.astype(jnp.int32)
            last_sub = sub
            found[jnp.maximum(slot, 0)] = sub
            jobs.append((_block_product(block_ref, index, steps), fresh, jnp.where(real, slot, trash)))
        for product, fresh, where in jobs:
            sums[where] = jnp.where(fresh, 0.0, sums[where]) + product
        return last_sub, slot

    _, top = lax.fori_loop(
        0, (count + UNROLL - 1) // UNROLL, grid_blocks, (jnp.int32(-1), jnp.int32(-1))
    )
    touched = top + 1

    def place_subs(step, carry):
        pieces = []
        for k in range(FFT_UNROLL):
            at = step * FFT_UNROLL + k
            real = at < touched
            at = jnp.minimum(at, touched - 1)
            sub = found[at]
            corner_u, corner_v, plane = place_ref[sub], place_ref[subs + sub], place_ref[2 * subs + sub]
            image = _combine(sums[at], sign)
            masked = image * screen_a_ref[plane] + pltpu.roll(image, SG, 1) * screen_b_ref[plane]
            hi, lo = _split(masked)
            wide = jnp.dot(
                jnp.concatenate([hi, lo], axis=1), right_ref[...], preferred_element_type=jnp.float32
            )
            half = wide[:, :LANES] + wide[:, LANES:]
            hi, lo = _split(half)
            four = jnp.dot(
                left_ref[...],
                jnp.concatenate([hi, lo, hi, jnp.zeros_like(hi)], axis=0),
                preferred_element_type=jnp.float32,
            )
            spectrum = _combine(four, sign)
            off_v = corner_v & (FV - 1)
            pieces.append((spectrum, real, corner_u & (FU - 1), off_v >> 7, off_v & (LANES - 1)))
        for spectrum, real, off_u, tile, s in pieces:
            turned = pltpu.roll(spectrum, s, 1)
            other = pltpu.roll(turned, SG, 1)
            begin = jnp.where(real, s, LANES)
            end = jnp.where(real, s + SG, 0)
            first = (lane >= begin) & (lane < end)
            second = lane < end - LANES
            rows = pl.ds(off_u, SG)
            for part, value in ((0, turned), (1, other)):
                facet[part, tile, rows, :] += jnp.where(first, value, 0.0)
                facet[part, tile + 1, rows, :] += jnp.where(second, value, 0.0)
        return carry

    lax.fori_loop(0, (touched + FFT_UNROLL - 1) // FFT_UNROLL, place_subs, 0)
    half = TILES // 2
    own = vis_ref[0] * half
    far = (1 - vis_ref[0]) * half
    for part in range(2):
        for t in range(half):
            mine_ref[part, :, t * LANES : (t + 1) * LANES] = facet[part, own + t]
            theirs_ref[part, :, t * LANES : (t + 1) * LANES] = facet[part, far + t]


def dft_tables():
    k = np.arange(SG)
    angle = 2.0 * np.pi * (np.outer(k, k) % SG) / SG
    re, im = np.cos(angle), -np.sin(angle)
    right = np.block([[re, im], [-im, re]]) / (SG * math.sqrt(BV))
    left = np.concatenate([re, im], axis=0)

    def split(x):
        hi = np.asarray(x, jnp.bfloat16).astype(np.float64)
        return hi, x - hi

    rhi, rlo = split(right)
    lhi, llo = split(left)
    right = np.block([[rhi, rlo], [rhi, np.zeros_like(rlo)]])
    left = np.concatenate([lhi, lhi, llo, np.zeros_like(llo)], axis=1)
    return jnp.asarray(right, jnp.bfloat16), jnp.asarray(left, jnp.bfloat16)


def on_device(
    visibilities,
    coords,
    block_subgrid,
    baseline_ids,
    live_blocks,
    subgrid_place,
    baseline_weight,
    tapering,
    plane_phase,
):
    nblocks = visibilities.shape[0]
    n_col = lax.axis_size("col")
    n_row = lax.axis_size("row")
    n_vis = lax.axis_size("vis")
    devices = n_col * n_row * n_vis
    facets = n_col * n_row
    sub_dev = subgrid_place.shape[1]
    subs = devices * sub_dev
    held = facets * nblocks
    max_subs = min(devices * (2 * sub_dev // facets), held)
    vis = lax.axis_index("vis")
    live = jnp.arange(nblocks) < live_blocks[0]

    label = jnp.where(live, block_subgrid, -1)
    meta = jnp.concatenate([label, subgrid_place.reshape(-1)])
    meta = lax.all_gather(meta, ("col", "row", "vis"), axis=0, tiled=False)

    weight = jnp.where(live, jnp.take(baseline_weight, baseline_ids), 0.0)
    weighted = visibilities.astype(jnp.float32) * weight[:, None, None]
    payload = jnp.concatenate([weighted, coords], axis=1).reshape(nblocks, 8, LANES)
    blocks = lax.all_gather(payload, ("col", "row"), axis=0, tiled=True)

    labels = lax.dynamic_index_in_dim(
        meta.reshape(facets, n_vis, -1), vis, axis=1, keepdims=False
    )[:, :nblocks].reshape(held)
    place = meta[:, nblocks:].reshape(devices, 3, sub_dev).transpose(1, 0, 2).reshape(3, subs)
    here = (place[0] // FU == lax.axis_index("col")) & (place[1] // FV == lax.axis_index("row"))
    wanted = (labels >= 0) & jnp.take(here, jnp.maximum(labels, 0))
    shift = max(1, (held - 1).bit_length())
    keys = jnp.where(wanted, (labels << shift) + jnp.arange(held, dtype=jnp.int32), BIG)
    keys = jnp.concatenate([lax.sort(keys), jnp.full((UNROLL,), BIG, jnp.int32)])
    count = jnp.sum(wanted.astype(jnp.int32)).reshape(1)

    screen_re = tapering * jnp.cos(plane_phase)
    screen_im = tapering * jnp.sin(plane_phase)
    screen_a = jnp.concatenate([screen_re, screen_re], axis=2)
    screen_b = jnp.concatenate([-screen_im, screen_im], axis=2)
    right, left = dft_tables()

    smem = pl.BlockSpec(memory_space=pltpu.SMEM)
    vmem = pl.BlockSpec(memory_space=pltpu.VMEM)
    half_shape = jax.ShapeDtypeStruct((2, FU, FV // n_vis), jnp.float32)
    mine, theirs = pl.pallas_call(
        functools.partial(facet_kernel, shift, subs),
        out_shape=(half_shape, half_shape),
        in_specs=[smem] * 4 + [vmem] * 5,
        out_specs=(vmem, vmem),
        scratch_shapes=[
            pltpu.VMEM((max_subs + 1, 2 * SG, 2 * SG), jnp.float32),
            pltpu.VMEM((2, TILES + 1, FU, LANES), jnp.float32),
            pltpu.SMEM((max_subs + 8,), jnp.int32),
        ],
        compiler_params=pltpu.CompilerParams(vmem_limit_bytes=56 * 1024 * 1024),
        name="facet",
    )(count, keys, place.reshape(-1), vis.reshape(1), blocks, screen_a, screen_b, right, left)
    swap = [(d, 1 - d) for d in range(n_vis)]
    return mine + lax.ppermute(theirs, "vis", swap)


def solution(mesh):
    spread = ("band", "col", "row", "vis")
    in_specs = (
        P(spread, None, None),
        P(spread, None, None),
        P(spread),
        P(spread),
        P(spread),
        P(None, spread),
        P(),
        P(),
        P(),
    )
    out_specs = P(None, ("band", "col"), ("row", "vis"))
    return jax.shard_map(
        on_device, mesh=mesh, in_specs=in_specs, out_specs=out_specs, check_vma=False
    )
```

```python
import functools
import math

import jax
import jax.numpy as jnp
import numpy as np
from jax import lax
from jax.experimental import pallas as pl
from jax.experimental.pallas import tpu as pltpu
from jax.sharding import PartitionSpec as P

SG = 64
BV = 256
FU = 512
FV = 512
LANES = 128
TILES = FV // LANES
UNROLL = 4
FFT_UNROLL = 4
BIG = 1 << 30


def _poly(fn, terms):
    y = np.cos(np.pi * (np.arange(400) + 0.5) / 400)
    s = 0.25 * 0.5 * (y + 1.0)
    fit = np.polynomial.chebyshev.Chebyshev.fit(s, fn(np.sqrt(s)), terms - 1, domain=[0.0, 0.25])
    return [float(c) for c in fit.convert(kind=np.polynomial.Polynomial, domain=[-1, 1]).coef]


COS_COEF = _poly(lambda t: np.cos(2 * np.pi * t), 8)
SIN_COEF = _poly(lambda t: np.sin(2 * np.pi * t) / t, 7)


def _horner(coef, s):
    out = jnp.full_like(s, coef[-1])
    for c in coef[-2::-1]:
        out = out * s + c
    return out


def _fine(turns, steps):
    t = turns * steps
    t = t - jnp.round(t)
    s = t * t
    return _horner(COS_COEF, s), t * _horner(SIN_COEF, s)


def _powers(turns, steps, scale):
    er, ei = _fine(turns, steps)
    z4r = jnp.broadcast_to(er[4:5], er.shape)
    z4i = jnp.broadcast_to(ei[4:5], ei.shape)

    def square(r, i):
        return r * r - i * i, 2.0 * (r * i)

    z1 = square(z4r, z4i)
    z2 = square(*z1)
    z3 = (z1[0] * z2[0] - z1[1] * z2[1], z1[0] * z2[1] + z1[1] * z2[0])
    z4 = square(*z2)
    if scale is not None:
        wr, wi = scale
        er, ei = er * wr - ei * wi, er * wi + ei * wr
    real = [None] * 8
    imag = [None] * 8
    real[4], imag[4] = er, ei
    for a, (zr, zi) in ((1, z1), (2, z2), (3, z3), (4, z4)):
        rr, ii, ri, ir = er * zr, ei * zi, er * zi, ei * zr
        real[4 - a], imag[4 - a] = rr + ii, ir - ri
        if a < 4:
            real[4 + a], imag[4 + a] = rr - ii, ri + ir
    return jnp.concatenate(real + imag, axis=0).astype(jnp.bfloat16)


def _block_product(block_ref, index, steps):
    left, right = [], []
    for h in range(2):
        def row(k):
            return jnp.broadcast_to(block_ref[index, 2 * k + h : 2 * k + h + 1, :], (8, LANES))

        left.append(_powers(row(2), steps, (row(0), row(1))))
        right.append(_powers(row(3), steps, None))
    return lax.dot_general(
        jnp.concatenate(left, axis=1),
        jnp.concatenate(right, axis=1),
        (((1,), (1,)), ((), ())),
        preferred_element_type=jnp.float32,
    )


def _split(x):
    hi = x.astype(jnp.bfloat16)
    lo = (x - hi.astype(jnp.float32)).astype(jnp.bfloat16)
    return hi, lo


def _combine(four, sign):
    return four[:SG] + pltpu.roll(four[SG:], SG, 1) * sign


def facet_kernel(
    shift,
    subs,
    count_ref,
    keys_ref,
    place_ref,
    vis_ref,
    block_ref,
    screen_a_ref,
    screen_b_ref,
    right_ref,
    left_ref,
    mine_ref,
    theirs_ref,
    sums,
    facet,
    found,
):
    trash = sums.shape[0] - 1
    steps = lax.broadcasted_iota(jnp.int32, (8, LANES), 0).astype(jnp.float32)
    lane = lax.broadcasted_iota(jnp.int32, (SG, LANES), 1)
    sign = jnp.where(lane < SG, -1.0, 1.0)
    facet[...] = jnp.zeros_like(facet)
    count = count_ref[0]

    def grid_blocks(step, carry):
        last_sub, slot = carry
        jobs = []
        for k in range(UNROLL):
            at = step * UNROLL + k
            key = keys_ref[at]
            real = at < count
            index = jnp.where(real, key & ((1 << shift) - 1), 0)
            sub = jnp.where(real, key >> shift, last_sub)
            fresh = sub != last_sub
            slot = slot + fresh.astype(jnp.int32)
            last_sub = sub
            found[jnp.maximum(slot, 0)] = sub
            jobs.append((_block_product(block_ref, index, steps), fresh, jnp.where(real, slot, trash)))
        for product, fresh, where in jobs:
            sums[where] = jnp.where(fresh, 0.0, sums[where]) + product
        return last_sub, slot

    _, top = lax.fori_loop(
        0, (count + UNROLL - 1) // UNROLL, grid_blocks, (jnp.int32(-1), jnp.int32(-1))
    )
    touched = top + 1

    def place_subs(step, carry):
        pieces = []
        for k in range(FFT_UNROLL):
            at = step * FFT_UNROLL + k
            real = at < touched
            at = jnp.minimum(at, touched - 1)
            sub = found[at]
            corner_u, corner_v, plane = place_ref[sub], place_ref[subs + sub], place_ref[2 * subs + sub]
            image = _combine(sums[at], sign)
            masked = image * screen_a_ref[plane] + pltpu.roll(image, SG, 1) * screen_b_ref[plane]
            hi, lo = _split(masked)
            wide = jnp.dot(
                jnp.concatenate([hi, lo], axis=1), right_ref[...], preferred_element_type=jnp.float32
            )
            half = wide[:, :LANES] + wide[:, LANES:]
            hi, lo = _split(half)
            four = jnp.dot(
                left_ref[...],
                jnp.concatenate([hi, lo, hi, jnp.zeros_like(hi)], axis=0),
                preferred_element_type=jnp.float32,
            )
            spectrum = _combine(four, sign)
            off_v = corner_v & (FV - 1)
            pieces.append((spectrum, real, corner_u & (FU - 1), off_v >> 7, off_v & (LANES - 1)))
        for spectrum, real, off_u, tile, s in pieces:
            turned = pltpu.roll(spectrum, s, 1)
            other = pltpu.roll(turned, SG, 1)
            begin = jnp.where(real, s, LANES)
            end = jnp.where(real, s + SG, 0)
            first = (lane >= begin) & (lane < end)
            second = lane < end - LANES
            rows = pl.ds(off_u, SG)
            for part, value in ((0, turned), (1, other)):
                facet[part, tile, rows, :] += jnp.where(first, value, 0.0)
                facet[part, tile + 1, rows, :] += jnp.where(second, value, 0.0)
        return carry

    lax.fori_loop(0, (touched + FFT_UNROLL - 1) // FFT_UNROLL, place_subs, 0)
    half = TILES // 2
    own = vis_ref[0] * half
    far = (1 - vis_ref[0]) * half
    for part in range(2):
        for t in range(half):
            mine_ref[part, :, t * LANES : (t + 1) * LANES] = facet[part, own + t]
            theirs_ref[part, :, t * LANES : (t + 1) * LANES] = facet[part, far + t]


def gather_kernel(n_col, n_row, mine_ref, out_ref, ring_send, ring_recv, row_send, row_recv, own_sem):
    col, row = lax.axis_index("col"), lax.axis_index("row")
    right, left = lax.rem(col + 1, n_col), lax.rem(col + n_col - 1, n_col)
    size = mine_ref.shape[0]
    mesh_ids = pl.DeviceIdType.MESH
    barrier = pltpu.get_barrier_semaphore()
    for peer in (left, right):
        pl.semaphore_signal(barrier, inc=1, device_id={"col": peer}, device_id_type=mesh_ids)
    for j in range(1, n_row):
        pl.semaphore_signal(
            barrier, inc=1, device_id={"row": lax.rem(row + j, n_row)}, device_id_type=mesh_ids
        )
    pl.semaphore_wait(barrier, 1 + n_row)

    def slot(back, at_row):
        source = lax.rem(col + n_col - back, n_col) * n_row + at_row
        return out_ref.at[pl.ds(source * size, size)]

    def ring(step):
        return pltpu.make_async_remote_copy(
            src_ref=mine_ref if step == 0 else slot(step, row),
            dst_ref=slot(step, row),
            send_sem=ring_send.at[step],
            recv_sem=ring_recv.at[step],
            device_id={"col": right},
            device_id_type=mesh_ids,
        )

    def across(step, j):
        return pltpu.make_async_remote_copy(
            src_ref=mine_ref if step == 0 else slot(step, row),
            dst_ref=slot(step, row),
            send_sem=row_send.at[step, j - 1],
            recv_sem=row_recv.at[step, j - 1],
            device_id={"row": lax.rem(row + j, n_row)},
            device_id_type=mesh_ids,
        )

    sent = []
    for step in range(n_col):
        if step < n_col - 1:
            copy = ring(step)
            copy.start()
            sent.append(copy)
        for j in range(1, n_row):
            side = across(step, j)
            side.start()
            sent.append(side)
        if step == 0:
            own = pltpu.make_async_copy(mine_ref, slot(0, row), own_sem)
            own.start()
        if step < n_col - 1:
            copy.wait_recv()
    own.wait()
    for copy in sent:
        copy.wait_send()
    for step in range(n_col):
        for j in range(1, n_row):
            across(step, j).wait_recv()


def gather_blocks(payload, n_col, n_row):
    size = payload.shape[0]
    hbm = pl.BlockSpec(memory_space=pl.ANY)
    return pl.pallas_call(
        functools.partial(gather_kernel, n_col, n_row),
        out_shape=jax.ShapeDtypeStruct((n_col * n_row * size,) + payload.shape[1:], payload.dtype),
        in_specs=[hbm],
        out_specs=hbm,
        scratch_shapes=[
            pltpu.SemaphoreType.DMA((n_col - 1,)),
            pltpu.SemaphoreType.DMA((n_col - 1,)),
            pltpu.SemaphoreType.DMA((n_col, n_row - 1)),
            pltpu.SemaphoreType.DMA((n_col, n_row - 1)),
            pltpu.SemaphoreType.DMA,
        ],
        compiler_params=pltpu.CompilerParams(collective_id=0, has_side_effects=True),
        name="gather",
    )(payload)


def dft_tables():
    k = np.arange(SG)
    angle = 2.0 * np.pi * (np.outer(k, k) % SG) / SG
    re, im = np.cos(angle), -np.sin(angle)
    right = np.block([[re, im], [-im, re]]) / (SG * math.sqrt(BV))
    left = np.concatenate([re, im], axis=0)

    def split(x):
        hi = np.asarray(x, jnp.bfloat16).astype(np.float64)
        return hi, x - hi

    rhi, rlo = split(right)
    lhi, llo = split(left)
    right = np.block([[rhi, rlo], [rhi, np.zeros_like(rlo)]])
    left = np.concatenate([lhi, lhi, llo, np.zeros_like(llo)], axis=1)
    return jnp.asarray(right, jnp.bfloat16), jnp.asarray(left, jnp.bfloat16)


def on_device(
    visibilities,
    coords,
    block_subgrid,
    baseline_ids,
    live_blocks,
    subgrid_place,
    baseline_weight,
    tapering,
    plane_phase,
):
    nblocks = visibilities.shape[0]
    n_col = lax.axis_size("col")
    n_row = lax.axis_size("row")
    n_vis = lax.axis_size("vis")
    devices = n_col * n_row * n_vis
    facets = n_col * n_row
    sub_dev = subgrid_place.shape[1]
    subs = devices * sub_dev
    held = facets * nblocks
    max_subs = min(devices * (2 * sub_dev // facets), held)
    vis = lax.axis_index("vis")
    live = jnp.arange(nblocks) < live_blocks[0]

    swap = [(d, n_vis - 1 - d) for d in range(n_vis)]
    label = jnp.where(live, block_subgrid, -1)
    meta = jnp.concatenate([label, subgrid_place.reshape(-1)]).astype(jnp.float32)
    meta = jnp.pad(meta, (0, 8 * LANES - meta.shape[0])).reshape(1, 8, LANES)
    other = lax.ppermute(meta, "vis", swap)
    pair = jnp.where(vis == 0, jnp.concatenate([meta, other]), jnp.concatenate([other, meta]))

    weight = jnp.where(live, jnp.take(baseline_weight, baseline_ids), 0.0)
    weighted = visibilities.astype(jnp.float32) * weight[:, None, None]
    payload = jnp.concatenate([weighted, coords], axis=1).reshape(nblocks, 8, LANES)
    stride = nblocks + n_vis
    blocks = gather_blocks(jnp.concatenate([payload, pair]), n_col, n_row)

    meta = blocks.reshape(facets, stride, 8, LANES)[:, nblocks:].astype(jnp.int32)
    meta = meta.reshape(facets, n_vis, 8 * LANES)
    labels = lax.dynamic_index_in_dim(meta, vis, axis=1, keepdims=False)[:, :nblocks]
    labels = labels.reshape(held)
    place = meta.reshape(devices, -1)[:, nblocks : nblocks + 3 * sub_dev]
    place = place.reshape(devices, 3, sub_dev).transpose(1, 0, 2).reshape(3, subs)
    here = (place[0] // FU == lax.axis_index("col")) & (place[1] // FV == lax.axis_index("row"))
    wanted = (labels >= 0) & jnp.take(here, jnp.maximum(labels, 0))
    index = jnp.arange(facets)[:, None] * stride + jnp.arange(nblocks)[None, :]
    index = index.reshape(held).astype(jnp.int32)
    shift = max(1, (facets * stride - 1).bit_length())
    keys = jnp.where(wanted, (labels << shift) + index, BIG)
    keys = jnp.concatenate([lax.sort(keys), jnp.full((UNROLL,), BIG, jnp.int32)])
    count = jnp.sum(wanted.astype(jnp.int32)).reshape(1)

    screen_re = tapering * jnp.cos(plane_phase)
    screen_im = tapering * jnp.sin(plane_phase)
    screen_a = jnp.concatenate([screen_re, screen_re], axis=2)
    screen_b = jnp.concatenate([-screen_im, screen_im], axis=2)
    right, left = dft_tables()

    smem = pl.BlockSpec(memory_space=pltpu.SMEM)
    vmem = pl.BlockSpec(memory_space=pltpu.VMEM)
    half_shape = jax.ShapeDtypeStruct((2, FU, FV // n_vis), jnp.float32)
    mine, theirs = pl.pallas_call(
        functools.partial(facet_kernel, shift, subs),
        out_shape=(half_shape, half_shape),
        in_specs=[smem] * 4 + [vmem] * 5,
        out_specs=(vmem, vmem),
        scratch_shapes=[
            pltpu.VMEM((max_subs + 1, 2 * SG, 2 * SG), jnp.float32),
            pltpu.VMEM((2, TILES + 1, FU, LANES), jnp.float32),
            pltpu.SMEM((max_subs + 8,), jnp.int32),
        ],
        compiler_params=pltpu.CompilerParams(vmem_limit_bytes=56 * 1024 * 1024),
        name="facet",
    )(count, keys, place.reshape(-1), vis.reshape(1), blocks, screen_a, screen_b, right, left)
    return mine + lax.ppermute(theirs, "vis", swap)


def solution(mesh):
    spread = ("band", "col", "row", "vis")
    in_specs = (
        P(spread, None, None),
        P(spread, None, None),
        P(spread),
        P(spread),
        P(spread),
        P(None, spread),
        P(),
        P(),
        P(),
    )
    out_specs = P(None, ("band", "col"), ("row", "vis"))
    return jax.shard_map(
        on_device, mesh=mesh, in_specs=in_specs, out_specs=out_specs, check_vma=False
    )
```

```python
import functools
import math

import jax
import jax.numpy as jnp
import numpy as np
from jax import lax
from jax.experimental import pallas as pl
from jax.experimental.pallas import tpu as pltpu
from jax.sharding import PartitionSpec as P

SG = 64
BV = 256
FU = 512
FV = 512
LANES = 128
TILES = FV // LANES
UNROLL = 16
FFT_UNROLL = 16
BIG = 1 << 30


def _poly(fn, terms):
    y = np.cos(np.pi * (np.arange(400) + 0.5) / 400)
    s = 0.25 * 0.5 * (y + 1.0)
    fit = np.polynomial.chebyshev.Chebyshev.fit(s, fn(np.sqrt(s)), terms - 1, domain=[0.0, 0.25])
    return [float(c) for c in fit.convert(kind=np.polynomial.Polynomial, domain=[-1, 1]).coef]


COS_COEF = _poly(lambda t: np.cos(2 * np.pi * t), 8)
SIN_COEF = _poly(lambda t: np.sin(2 * np.pi * t) / t, 7)


def _horner(coef, s):
    out = jnp.full_like(s, coef[-1])
    for c in coef[-2::-1]:
        out = out * s + c
    return out


def _fine(turns, steps):
    t = turns * steps
    t = t - jnp.round(t)
    s = t * t
    return _horner(COS_COEF, s), t * _horner(SIN_COEF, s)


def _powers(turns, steps, scale):
    er, ei = _fine(turns, steps)
    z4r = jnp.broadcast_to(er[4:5], er.shape)
    z4i = jnp.broadcast_to(ei[4:5], ei.shape)

    def square(r, i):
        return r * r - i * i, 2.0 * (r * i)

    z1 = square(z4r, z4i)
    z2 = square(*z1)
    z3 = (z1[0] * z2[0] - z1[1] * z2[1], z1[0] * z2[1] + z1[1] * z2[0])
    z4 = square(*z2)
    if scale is not None:
        wr, wi = scale
        er, ei = er * wr - ei * wi, er * wi + ei * wr
    real = [None] * 8
    imag = [None] * 8
    real[4], imag[4] = er, ei
    for a, (zr, zi) in ((1, z1), (2, z2), (3, z3), (4, z4)):
        rr, ii, ri, ir = er * zr, ei * zi, er * zi, ei * zr
        real[4 - a], imag[4 - a] = rr + ii, ir - ri
        if a < 4:
            real[4 + a], imag[4 + a] = rr - ii, ri + ir
    return jnp.concatenate(real + imag, axis=0).astype(jnp.bfloat16)


def _block_product(block_ref, index, steps):
    left, right = [], []
    for h in range(2):
        def row(k):
            return jnp.broadcast_to(block_ref[index, 2 * k + h : 2 * k + h + 1, :], (8, LANES))

        left.append(_powers(row(2), steps, (row(0), row(1))))
        right.append(_powers(row(3), steps, None))
    return lax.dot_general(
        jnp.concatenate(left, axis=1),
        jnp.concatenate(right, axis=1),
        (((1,), (1,)), ((), ())),
        preferred_element_type=jnp.float32,
    )


def _split(x):
    hi = x.astype(jnp.bfloat16)
    lo = (x - hi.astype(jnp.float32)).astype(jnp.bfloat16)
    return hi, lo


def _combine(four, sign):
    return four[:SG] + pltpu.roll(four[SG:], SG, 1) * sign


def facet_kernel(
    shift,
    subs,
    count_ref,
    keys_ref,
    place_ref,
    vis_ref,
    block_ref,
    screen_a_ref,
    screen_b_ref,
    right_ref,
    left_ref,
    mine_ref,
    theirs_ref,
    sums,
    facet,
    found,
):
    trash = sums.shape[0] - 1
    steps = lax.broadcasted_iota(jnp.int32, (8, LANES), 0).astype(jnp.float32)
    lane = lax.broadcasted_iota(jnp.int32, (SG, LANES), 1)
    sign = jnp.where(lane < SG, -1.0, 1.0)
    facet[...] = jnp.zeros_like(facet)
    count = count_ref[0]

    def grid_blocks(step, carry):
        last_sub, slot = carry
        jobs = []
        for k in range(UNROLL):
            at = step * UNROLL + k
            key = keys_ref[at]
            real = at < count
            index = jnp.where(real, key & ((1 << shift) - 1), 0)
            sub = jnp.where(real, key >> shift, last_sub)
            fresh = sub != last_sub
            slot = slot + fresh.astype(jnp.int32)
            last_sub = sub
            found[jnp.maximum(slot, 0)] = sub
            jobs.append((_block_product(block_ref, index, steps), fresh, jnp.where(real, slot, trash)))
        for product, fresh, where in jobs:
            sums[where] = jnp.where(fresh, 0.0, sums[where]) + product
        return last_sub, slot

    _, top = lax.fori_loop(
        0, (count + UNROLL - 1) // UNROLL, grid_blocks, (jnp.int32(-1), jnp.int32(-1))
    )
    touched = top + 1

    def place_subs(step, carry):
        pieces = []
        for k in range(FFT_UNROLL):
            at = step * FFT_UNROLL + k
            real = at < touched
            at = jnp.minimum(at, touched - 1)
            sub = found[at]
            corner_u, corner_v, plane = place_ref[sub], place_ref[subs + sub], place_ref[2 * subs + sub]
            image = _combine(sums[at], sign)
            masked = image * screen_a_ref[plane] + pltpu.roll(image, SG, 1) * screen_b_ref[plane]
            hi, lo = _split(masked)
            wide = jnp.dot(
                jnp.concatenate([hi, lo], axis=1), right_ref[...], preferred_element_type=jnp.float32
            )
            half = wide[:, :LANES] + wide[:, LANES:]
            hi, lo = _split(half)
            four = jnp.dot(
                left_ref[...],
                jnp.concatenate([hi, lo, hi, jnp.zeros_like(hi)], axis=0),
                preferred_element_type=jnp.float32,
            )
            spectrum = _combine(four, sign)
            off_v = corner_v & (FV - 1)
            pieces.append((spectrum, real, corner_u & (FU - 1), off_v >> 7, off_v & (LANES - 1)))
        for spectrum, real, off_u, tile, s in pieces:
            turned = pltpu.roll(spectrum, s, 1)
            other = pltpu.roll(turned, SG, 1)
            begin = jnp.where(real, s, LANES)
            end = jnp.where(real, s + SG, 0)
            first = (lane >= begin) & (lane < end)
            second = lane < end - LANES
            rows = pl.ds(off_u, SG)
            spots = [(part, tile + t, rows) for part in range(2) for t in range(2)]
            before = [facet[spot] for spot in spots]
            parts = [jnp.where(m, v, 0.0) for v in (turned, other) for m in (first, second)]
            for spot, old, new in zip(spots, before, parts):
                facet[spot] = old + new
        return carry

    lax.fori_loop(0, (touched + FFT_UNROLL - 1) // FFT_UNROLL, place_subs, 0)
    half = TILES // 2
    own = vis_ref[0] * half
    far = (1 - vis_ref[0]) * half
    for part in range(2):
        for t in range(half):
            mine_ref[part, :, t * LANES : (t + 1) * LANES] = facet[part, own + t]
            theirs_ref[part, :, t * LANES : (t + 1) * LANES] = facet[part, far + t]


def gather_kernel(n_col, n_row, chunks, mine_ref, out_ref, ring_send, ring_recv, row_send, row_recv, own_sem):
    col, row = lax.axis_index("col"), lax.axis_index("row")
    right, left = lax.rem(col + 1, n_col), lax.rem(col + n_col - 1, n_col)
    size = mine_ref.shape[0]
    mesh_ids = pl.DeviceIdType.MESH
    barrier = pltpu.get_barrier_semaphore()
    for peer in (left, right):
        pl.semaphore_signal(barrier, inc=1, device_id={"col": peer}, device_id_type=mesh_ids)
    for j in range(1, n_row):
        pl.semaphore_signal(
            barrier, inc=1, device_id={"row": lax.rem(row + j, n_row)}, device_id_type=mesh_ids
        )
    pl.semaphore_wait(barrier, 1 + n_row)

    def slot(back, at_row, k):
        source = lax.rem(col + n_col - back, n_col) * n_row + at_row
        first, count = chunks[k]
        return out_ref.at[pl.ds(source * size + first, count)]

    def from_here(step, at_row, k):
        first, count = chunks[k]
        return mine_ref.at[pl.ds(first, count)] if step == 0 else slot(step, at_row, k)

    def ring(step, j, k):
        at_row = lax.rem(row + j, n_row)
        return pltpu.make_async_remote_copy(
            src_ref=from_here(step, at_row, k) if j == 0 else slot(step, at_row, k),
            dst_ref=slot(step, at_row, k),
            send_sem=ring_send.at[step, j, k],
            recv_sem=ring_recv.at[step, j, k],
            device_id={"col": right},
            device_id_type=mesh_ids,
        )

    def across(step, j, k):
        return pltpu.make_async_remote_copy(
            src_ref=from_here(step, row, k),
            dst_ref=slot(step, row, k),
            send_sem=row_send.at[step, j - 1, k],
            recv_sem=row_recv.at[step, j - 1, k],
            device_id={"row": lax.rem(row + j, n_row)},
            device_id_type=mesh_ids,
        )

    sent = []

    def start(copy):
        copy.start()
        sent.append(copy)

    others = range(1, n_row)
    late = range(1, len(chunks))
    for j in others:
        start(across(0, j, 0))
    for k in range(len(chunks)):
        start(ring(0, 0, k))
    own = pltpu.make_async_copy(
        mine_ref, out_ref.at[pl.ds((col * n_row + row) * size, size)], own_sem
    )
    own.start()
    for k in late:
        for j in others:
            start(across(0, j, k))
    for j in others:
        across(0, n_row - j, 0).wait_recv()
        start(ring(0, j, 0))
    for step in range(1, n_col):
        for k in late:
            ring(step - 1, 0, k).wait_recv()
            if step < n_col - 1:
                start(ring(step, 0, k))
            for j in others:
                start(across(step, j, k))
        for j in range(n_row):
            ring(step - 1, j, 0).wait_recv()
            if step < n_col - 1:
                start(ring(step, j, 0))
    own.wait()
    for copy in sent:
        copy.wait_send()
    for step in range(n_col):
        for k in late:
            for j in others:
                across(step, j, k).wait_recv()


def gather_blocks(payload, n_col, n_row):
    size = payload.shape[0]
    early = size // 6
    ends = [0] + [early + (size - early) * k // 4 for k in range(5)]
    chunks = [(ends[k], ends[k + 1] - ends[k]) for k in range(5)]
    hbm = pl.BlockSpec(memory_space=pl.ANY)
    return pl.pallas_call(
        functools.partial(gather_kernel, n_col, n_row, chunks),
        out_shape=jax.ShapeDtypeStruct((n_col * n_row * size,) + payload.shape[1:], payload.dtype),
        in_specs=[hbm],
        out_specs=hbm,
        scratch_shapes=[
            pltpu.SemaphoreType.DMA((n_col - 1, n_row, 5)),
            pltpu.SemaphoreType.DMA((n_col - 1, n_row, 5)),
            pltpu.SemaphoreType.DMA((n_col, n_row - 1, 5)),
            pltpu.SemaphoreType.DMA((n_col, n_row - 1, 5)),
            pltpu.SemaphoreType.DMA,
        ],
        compiler_params=pltpu.CompilerParams(collective_id=0, has_side_effects=True),
        name="gather",
    )(payload)


def dft_tables():
    k = np.arange(SG)
    angle = 2.0 * np.pi * (np.outer(k, k) % SG) / SG
    re, im = np.cos(angle), -np.sin(angle)
    right = np.block([[re, im], [-im, re]]) / (SG * math.sqrt(BV))
    left = np.concatenate([re, im], axis=0)

    def split(x):
        hi = np.asarray(x, jnp.bfloat16).astype(np.float64)
        return hi, x - hi

    rhi, rlo = split(right)
    lhi, llo = split(left)
    right = np.block([[rhi, rlo], [rhi, np.zeros_like(rlo)]])
    left = np.concatenate([lhi, lhi, llo, np.zeros_like(llo)], axis=1)
    return jnp.asarray(right, jnp.bfloat16), jnp.asarray(left, jnp.bfloat16)


def on_device(
    visibilities,
    coords,
    block_subgrid,
    baseline_ids,
    live_blocks,
    subgrid_place,
    baseline_weight,
    tapering,
    plane_phase,
):
    nblocks = visibilities.shape[0]
    n_col = lax.axis_size("col")
    n_row = lax.axis_size("row")
    n_vis = lax.axis_size("vis")
    devices = n_col * n_row * n_vis
    facets = n_col * n_row
    sub_dev = subgrid_place.shape[1]
    subs = devices * sub_dev
    held = facets * nblocks
    max_subs = min(devices * (2 * sub_dev // facets), held)
    vis = lax.axis_index("vis")
    live = jnp.arange(nblocks) < live_blocks[0]

    swap = [(d, n_vis - 1 - d) for d in range(n_vis)]
    label = jnp.where(live, block_subgrid, -1)
    meta = jnp.concatenate([label, subgrid_place.reshape(-1)]).astype(jnp.float32)
    meta = jnp.pad(meta, (0, 8 * LANES - meta.shape[0])).reshape(1, 8, LANES)
    other = lax.ppermute(meta, "vis", swap)
    pair = jnp.where(vis == 0, jnp.concatenate([meta, other]), jnp.concatenate([other, meta]))

    weight = jnp.where(live, jnp.take(baseline_weight, baseline_ids), 0.0)
    weighted = visibilities.astype(jnp.float32) * weight[:, None, None]
    payload = jnp.concatenate([weighted, coords], axis=1).reshape(nblocks, 8, LANES)
    stride = nblocks + n_vis
    blocks = gather_blocks(jnp.concatenate([payload, pair]), n_col, n_row)

    meta = blocks.reshape(facets, stride, 8, LANES)[:, nblocks:].astype(jnp.int32)
    meta = meta.reshape(facets, n_vis, 8 * LANES)
    labels = lax.dynamic_index_in_dim(meta, vis, axis=1, keepdims=False)[:, :nblocks]
    labels = labels.reshape(held)
    place = meta.reshape(devices, -1)[:, nblocks : nblocks + 3 * sub_dev].reshape(devices, 3, sub_dev)
    here = (place[:, 0] // FU == lax.axis_index("col")) & (place[:, 1] // FV == lax.axis_index("row"))
    place = place.transpose(1, 0, 2)
    owner = (labels[:, None] // sub_dev == jnp.arange(devices)).astype(jnp.float32)
    local = labels[:, None] % sub_dev == jnp.arange(sub_dev)
    named = jnp.dot(owner, here.astype(jnp.float32))
    wanted = (labels >= 0) & (jnp.sum(jnp.where(local, named, 0.0), axis=1) > 0.5)
    index = jnp.arange(facets)[:, None] * stride + jnp.arange(nblocks)[None, :]
    index = index.reshape(held).astype(jnp.int32)
    shift = max(1, (facets * stride - 1).bit_length())
    keys = jnp.where(wanted, (labels << shift) + index, BIG)
    keys = jnp.concatenate([lax.sort(keys), jnp.full((UNROLL,), BIG, jnp.int32)])
    count = jnp.sum(wanted.astype(jnp.int32)).reshape(1)

    screen_re = tapering * jnp.cos(plane_phase)
    screen_im = tapering * jnp.sin(plane_phase)
    screen_a = jnp.concatenate([screen_re, screen_re], axis=2)
    screen_b = jnp.concatenate([-screen_im, screen_im], axis=2)
    right, left = dft_tables()

    smem = pl.BlockSpec(memory_space=pltpu.SMEM)
    vmem = pl.BlockSpec(memory_space=pltpu.VMEM)
    half_shape = jax.ShapeDtypeStruct((2, FU, FV // n_vis), jnp.float32)
    mine, theirs = pl.pallas_call(
        functools.partial(facet_kernel, shift, subs),
        out_shape=(half_shape, half_shape),
        in_specs=[smem] * 4 + [vmem] * 5,
        out_specs=(vmem, vmem),
        scratch_shapes=[
            pltpu.VMEM((max_subs + 1, 2 * SG, 2 * SG), jnp.float32),
            pltpu.VMEM((2, TILES + 1, FU, LANES), jnp.float32),
            pltpu.SMEM((max_subs + 8,), jnp.int32),
        ],
        compiler_params=pltpu.CompilerParams(vmem_limit_bytes=56 * 1024 * 1024),
        name="facet",
    )(count, keys, place.reshape(-1), vis.reshape(1), blocks, screen_a, screen_b, right, left)
    return mine + lax.ppermute(theirs, "vis", swap)


def solution(mesh):
    spread = ("band", "col", "row", "vis")
    in_specs = (
        P(spread, None, None),
        P(spread, None, None),
        P(spread),
        P(spread),
        P(spread),
        P(None, spread),
        P(),
        P(),
        P(),
    )
    out_specs = P(None, ("band", "col"), ("row", "vis"))
    return jax.shard_map(
        on_device, mesh=mesh, in_specs=in_specs, out_specs=out_specs, check_vma=False
    )
```

```python
import functools
import math

import jax
import jax.numpy as jnp
import numpy as np
from jax import lax
from jax.experimental import pallas as pl
from jax.experimental.pallas import tpu as pltpu
from jax.sharding import PartitionSpec as P

SG = 64
BV = 256
FU = 512
FV = 512
LANES = 128
TILES = FV // LANES
UNROLL = 16
FFT_UNROLL = 16
BIG = 1 << 30


def _poly(fn, terms):
    y = np.cos(np.pi * (np.arange(400) + 0.5) / 400)
    s = 0.25 * 0.5 * (y + 1.0)
    fit = np.polynomial.chebyshev.Chebyshev.fit(s, fn(np.sqrt(s)), terms - 1, domain=[0.0, 0.25])
    return [float(c) for c in fit.convert(kind=np.polynomial.Polynomial, domain=[-1, 1]).coef]


COS_COEF = _poly(lambda t: np.cos(2 * np.pi * t), 8)
SIN_COEF = _poly(lambda t: np.sin(2 * np.pi * t) / t, 7)


def _horner(coef, s):
    out = jnp.full_like(s, coef[-1])
    for c in coef[-2::-1]:
        out = out * s + c
    return out


def _fine(turns, steps):
    t = turns * steps
    t = t - jnp.round(t)
    s = t * t
    return _horner(COS_COEF, s), t * _horner(SIN_COEF, s)


def _powers(turns, steps, scale):
    er, ei = _fine(turns, steps)
    z4r = jnp.broadcast_to(er[4:5], er.shape)
    z4i = jnp.broadcast_to(ei[4:5], ei.shape)

    def square(r, i):
        return r * r - i * i, 2.0 * (r * i)

    z1 = square(z4r, z4i)
    z2 = square(*z1)
    z3 = (z1[0] * z2[0] - z1[1] * z2[1], z1[0] * z2[1] + z1[1] * z2[0])
    z4 = square(*z2)
    if scale is not None:
        wr, wi = scale
        er, ei = er * wr - ei * wi, er * wi + ei * wr
    real = [None] * 8
    imag = [None] * 8
    real[4], imag[4] = er, ei
    for a, (zr, zi) in ((1, z1), (2, z2), (3, z3), (4, z4)):
        rr, ii, ri, ir = er * zr, ei * zi, er * zi, ei * zr
        real[4 - a], imag[4 - a] = rr + ii, ir - ri
        if a < 4:
            real[4 + a], imag[4 + a] = rr - ii, ri + ir
    return jnp.concatenate(real + imag, axis=0).astype(jnp.bfloat16)


def _block_product(block_ref, index, steps):
    left, right = [], []
    for h in range(2):
        def row(k):
            return jnp.broadcast_to(block_ref[index, 2 * k + h : 2 * k + h + 1, :], (8, LANES))

        left.append(_powers(row(2), steps, (row(0), row(1))))
        right.append(_powers(row(3), steps, None))
    return lax.dot_general(
        jnp.concatenate(left, axis=1),
        jnp.concatenate(right, axis=1),
        (((1,), (1,)), ((), ())),
        preferred_element_type=jnp.float32,
    )


def _split(x):
    hi = x.astype(jnp.bfloat16)
    lo = (x - hi.astype(jnp.float32)).astype(jnp.bfloat16)
    return hi, lo


def _combine(four, sign):
    return four[:SG] + pltpu.roll(four[SG:], SG, 1) * sign


def facet_kernel(
    shift,
    subs,
    count_ref,
    keys_ref,
    place_ref,
    vis_ref,
    block_ref,
    screen_a_ref,
    screen_b_ref,
    right_ref,
    left_ref,
    mine_ref,
    theirs_ref,
    sums,
    facet,
    found,
):
    trash = sums.shape[0] - 1
    steps = lax.broadcasted_iota(jnp.int32, (8, LANES), 0).astype(jnp.float32)
    lane = lax.broadcasted_iota(jnp.int32, (SG, LANES), 1)
    sign = jnp.where(lane < SG, -1.0, 1.0)
    facet[...] = jnp.zeros_like(facet)
    count = count_ref[0]

    def grid_blocks(step, carry):
        last_sub, slot = carry
        jobs = []
        for k in range(UNROLL):
            at = step * UNROLL + k
            key = keys_ref[jnp.minimum(at, keys_ref.shape[0] - 1)]
            real = at < count
            index = jnp.where(real, key & ((1 << shift) - 1), 0)
            sub = jnp.where(real, key >> shift, last_sub)
            fresh = sub != last_sub
            slot = slot + fresh.astype(jnp.int32)
            last_sub = sub
            found[jnp.maximum(slot, 0)] = sub
            jobs.append((_block_product(block_ref, index, steps), fresh, jnp.where(real, slot, trash)))
        for product, fresh, where in jobs:
            sums[where] = jnp.where(fresh, 0.0, sums[where]) + product
        return last_sub, slot

    _, top = lax.fori_loop(
        0, (count + UNROLL - 1) // UNROLL, grid_blocks, (jnp.int32(-1), jnp.int32(-1))
    )
    touched = top + 1

    def place_subs(step, carry):
        pieces = []
        for k in range(FFT_UNROLL):
            at = step * FFT_UNROLL + k
            real = at < touched
            at = jnp.minimum(at, touched - 1)
            sub = found[at]
            corner_u, corner_v, plane = place_ref[sub], place_ref[subs + sub], place_ref[2 * subs + sub]
            image = _combine(sums[at], sign)
            masked = image * screen_a_ref[plane] + pltpu.roll(image, SG, 1) * screen_b_ref[plane]
            hi, lo = _split(masked)
            wide = jnp.dot(
                jnp.concatenate([hi, lo], axis=1), right_ref[...], preferred_element_type=jnp.float32
            )
            half = wide[:, :LANES] + wide[:, LANES:]
            hi, lo = _split(half)
            four = jnp.dot(
                left_ref[...],
                jnp.concatenate([hi, lo, hi, jnp.zeros_like(hi)], axis=0),
                preferred_element_type=jnp.float32,
            )
            spectrum = _combine(four, sign)
            off_v = corner_v & (FV - 1)
            pieces.append((spectrum, real, corner_u & (FU - 1), off_v >> 7, off_v & (LANES - 1)))
        for spectrum, real, off_u, tile, s in pieces:
            turned = pltpu.roll(spectrum, s, 1)
            other = pltpu.roll(turned, SG, 1)
            begin = jnp.where(real, s, LANES)
            end = jnp.where(real, s + SG, 0)
            first = (lane >= begin) & (lane < end)
            second = lane < end - LANES
            rows = pl.ds(off_u, SG)
            spots = [(part, tile + t, rows) for part in range(2) for t in range(2)]
            before = [facet[spot] for spot in spots]
            parts = [jnp.where(m, v, 0.0) for v in (turned, other) for m in (first, second)]
            for spot, old, new in zip(spots, before, parts):
                facet[spot] = old + new
        return carry

    lax.fori_loop(0, (touched + FFT_UNROLL - 1) // FFT_UNROLL, place_subs, 0)
    half = TILES // 2
    own = vis_ref[0] * half
    far = (1 - vis_ref[0]) * half
    for part in range(2):
        for t in range(half):
            mine_ref[part, :, t * LANES : (t + 1) * LANES] = facet[part, own + t]
            theirs_ref[part, :, t * LANES : (t + 1) * LANES] = facet[part, far + t]


def gather_kernel(n_col, n_row, chunks, mine_ref, out_ref, ring_send, ring_recv, row_send, row_recv, own_sem):
    col, row = lax.axis_index("col"), lax.axis_index("row")
    right, left = lax.rem(col + 1, n_col), lax.rem(col + n_col - 1, n_col)
    size = mine_ref.shape[0]
    mesh_ids = pl.DeviceIdType.MESH
    barrier = pltpu.get_barrier_semaphore()
    for peer in (left, right):
        pl.semaphore_signal(barrier, inc=1, device_id={"col": peer}, device_id_type=mesh_ids)
    for j in range(1, n_row):
        pl.semaphore_signal(
            barrier, inc=1, device_id={"row": lax.rem(row + j, n_row)}, device_id_type=mesh_ids
        )
    pl.semaphore_wait(barrier, 1 + n_row)

    def slot(back, at_row, k):
        source = lax.rem(col + n_col - back, n_col) * n_row + at_row
        first, count = chunks[k]
        return out_ref.at[pl.ds(source * size + first, count)]

    def from_here(step, at_row, k):
        first, count = chunks[k]
        return mine_ref.at[pl.ds(first, count)] if step == 0 else slot(step, at_row, k)

    def ring(step, j, k):
        at_row = lax.rem(row + j, n_row)
        return pltpu.make_async_remote_copy(
            src_ref=from_here(step, at_row, k) if j == 0 else slot(step, at_row, k),
            dst_ref=slot(step, at_row, k),
            send_sem=ring_send.at[step, j, k],
            recv_sem=ring_recv.at[step, j, k],
            device_id={"col": right},
            device_id_type=mesh_ids,
        )

    def across(step, j, k):
        return pltpu.make_async_remote_copy(
            src_ref=from_here(step, row, k),
            dst_ref=slot(step, row, k),
            send_sem=row_send.at[step, j - 1, k],
            recv_sem=row_recv.at[step, j - 1, k],
            device_id={"row": lax.rem(row + j, n_row)},
            device_id_type=mesh_ids,
        )

    sent = []

    def start(copy):
        copy.start()
        sent.append(copy)

    others = range(1, n_row)
    late = range(1, len(chunks))
    for j in others:
        start(across(0, j, 0))
    for k in range(len(chunks)):
        start(ring(0, 0, k))
    own = pltpu.make_async_copy(
        mine_ref, out_ref.at[pl.ds((col * n_row + row) * size, size)], own_sem
    )
    own.start()
    for k in late:
        for j in others:
            start(across(0, j, k))
    for j in others:
        across(0, n_row - j, 0).wait_recv()
        start(ring(0, j, 0))
    for step in range(1, n_col):
        for k in late:
            ring(step - 1, 0, k).wait_recv()
            if step < n_col - 1:
                start(ring(step, 0, k))
            for j in others:
                start(across(step, j, k))
        for j in range(n_row):
            ring(step - 1, j, 0).wait_recv()
            if step < n_col - 1:
                start(ring(step, j, 0))
    own.wait()
    for copy in sent:
        copy.wait_send()
    for step in range(n_col):
        for k in late:
            for j in others:
                across(step, j, k).wait_recv()


def gather_blocks(payload, n_col, n_row):
    size = payload.shape[0]
    early = size // 6
    ends = [0] + [early + (size - early) * k // 4 for k in range(5)]
    chunks = [(ends[k], ends[k + 1] - ends[k]) for k in range(5)]
    hbm = pl.BlockSpec(memory_space=pl.ANY)
    return pl.pallas_call(
        functools.partial(gather_kernel, n_col, n_row, chunks),
        out_shape=jax.ShapeDtypeStruct((n_col * n_row * size,) + payload.shape[1:], payload.dtype),
        in_specs=[hbm],
        out_specs=hbm,
        scratch_shapes=[
            pltpu.SemaphoreType.DMA((n_col - 1, n_row, 5)),
            pltpu.SemaphoreType.DMA((n_col - 1, n_row, 5)),
            pltpu.SemaphoreType.DMA((n_col, n_row - 1, 5)),
            pltpu.SemaphoreType.DMA((n_col, n_row - 1, 5)),
            pltpu.SemaphoreType.DMA,
        ],
        compiler_params=pltpu.CompilerParams(collective_id=0, has_side_effects=True),
        name="gather",
    )(payload)


def dft_tables():
    k = np.arange(SG)
    angle = 2.0 * np.pi * (np.outer(k, k) % SG) / SG
    re, im = np.cos(angle), -np.sin(angle)
    right = np.block([[re, im], [-im, re]]) / (SG * math.sqrt(BV))
    left = np.concatenate([re, im], axis=0)

    def split(x):
        hi = np.asarray(x, jnp.bfloat16).astype(np.float64)
        return hi, x - hi

    rhi, rlo = split(right)
    lhi, llo = split(left)
    right = np.block([[rhi, rlo], [rhi, np.zeros_like(rlo)]])
    left = np.concatenate([lhi, lhi, llo, np.zeros_like(llo)], axis=1)
    return jnp.asarray(right, jnp.bfloat16), jnp.asarray(left, jnp.bfloat16)


def on_device(
    visibilities,
    coords,
    block_subgrid,
    baseline_ids,
    live_blocks,
    subgrid_place,
    baseline_weight,
    tapering,
    plane_phase,
):
    nblocks = visibilities.shape[0]
    n_col = lax.axis_size("col")
    n_row = lax.axis_size("row")
    n_vis = lax.axis_size("vis")
    devices = n_col * n_row * n_vis
    facets = n_col * n_row
    sub_dev = subgrid_place.shape[1]
    subs = devices * sub_dev
    held = facets * nblocks
    max_subs = min(devices * (2 * sub_dev // facets), held)
    vis = lax.axis_index("vis")
    live = jnp.arange(nblocks) < live_blocks[0]

    swap = [(d, n_vis - 1 - d) for d in range(n_vis)]
    label = jnp.where(live, block_subgrid, -1)
    meta = jnp.concatenate([label, subgrid_place.reshape(-1)]).astype(jnp.float32)
    meta = jnp.pad(meta, (0, 8 * LANES - meta.shape[0])).reshape(1, 8, LANES)
    other = lax.ppermute(meta, "vis", swap)
    pair = jnp.where(vis == 0, jnp.concatenate([meta, other]), jnp.concatenate([other, meta]))

    weight = jnp.where(live, jnp.take(baseline_weight, baseline_ids), 0.0)
    weighted = visibilities.astype(jnp.float32) * weight[:, None, None]
    payload = jnp.concatenate([weighted, coords], axis=1).reshape(nblocks, 8, LANES)
    stride = nblocks + n_vis
    blocks = gather_blocks(jnp.concatenate([payload, pair]), n_col, n_row)

    meta = blocks.reshape(facets, stride, 8, LANES)[:, nblocks:].astype(jnp.int32)
    meta = meta.reshape(facets, n_vis, 8 * LANES)
    labels = lax.dynamic_index_in_dim(meta, vis, axis=1, keepdims=False)[:, :nblocks]
    labels = labels.reshape(held)
    place = meta.reshape(devices, -1)[:, nblocks : nblocks + 3 * sub_dev].reshape(devices, 3, sub_dev)
    here = (place[:, 0] // FU == lax.axis_index("col")) & (place[:, 1] // FV == lax.axis_index("row"))
    place = place.transpose(1, 0, 2)
    owner = (labels[:, None] // sub_dev == jnp.arange(devices)).astype(jnp.float32)
    local = labels[:, None] % sub_dev == jnp.arange(sub_dev)
    named = jnp.dot(owner, here.astype(jnp.float32))
    wanted = (labels >= 0) & (jnp.sum(jnp.where(local, named, 0.0), axis=1) > 0.5)
    index = jnp.arange(facets)[:, None] * stride + jnp.arange(nblocks)[None, :]
    index = index.reshape(held).astype(jnp.int32)
    shift = max(1, (facets * stride - 1).bit_length())
    keys = jnp.where(wanted, (labels << shift) + index, BIG)
    keys = lax.sort(keys, is_stable=False)
    count = jnp.sum(wanted.astype(jnp.int32)).reshape(1)

    screen_re = tapering * jnp.cos(plane_phase)
    screen_im = tapering * jnp.sin(plane_phase)
    screen_a = jnp.concatenate([screen_re, screen_re], axis=2)
    screen_b = jnp.concatenate([-screen_im, screen_im], axis=2)
    right, left = dft_tables()

    smem = pl.BlockSpec(memory_space=pltpu.SMEM)
    vmem = pl.BlockSpec(memory_space=pltpu.VMEM)
    half_shape = jax.ShapeDtypeStruct((2, FU, FV // n_vis), jnp.float32)
    mine, theirs = pl.pallas_call(
        functools.partial(facet_kernel, shift, subs),
        out_shape=(half_shape, half_shape),
        in_specs=[smem] * 4 + [vmem] * 5,
        out_specs=(vmem, vmem),
        scratch_shapes=[
            pltpu.VMEM((max_subs + 1, 2 * SG, 2 * SG), jnp.float32),
            pltpu.VMEM((2, TILES + 1, FU, LANES), jnp.float32),
            pltpu.SMEM((max_subs + 8,), jnp.int32),
        ],
        compiler_params=pltpu.CompilerParams(vmem_limit_bytes=56 * 1024 * 1024),
        name="facet",
    )(count, keys, place.reshape(-1), vis.reshape(1), blocks, screen_a, screen_b, right, left)
    return mine + lax.ppermute(theirs, "vis", swap)


def solution(mesh):
    spread = ("band", "col", "row", "vis")
    in_specs = (
        P(spread, None, None),
        P(spread, None, None),
        P(spread),
        P(spread),
        P(spread),
        P(None, spread),
        P(),
        P(),
        P(),
    )
    out_specs = P(None, ("band", "col"), ("row", "vis"))
    return jax.shard_map(
        on_device, mesh=mesh, in_specs=in_specs, out_specs=out_specs, check_vma=False
    )
```

```python
import functools
import math

import jax
import jax.numpy as jnp
import numpy as np
from jax import lax
from jax.experimental import pallas as pl
from jax.experimental.pallas import tpu as pltpu
from jax.sharding import PartitionSpec as P

SG = 64
BV = 256
FU = 512
FV = 512
LANES = 128
TILES = FV // LANES
UNROLL = 16
FFT_UNROLL = 16
BIG = 1 << 30


def _poly(fn, terms):
    y = np.cos(np.pi * (np.arange(400) + 0.5) / 400)
    s = 0.25 * 0.5 * (y + 1.0)
    fit = np.polynomial.chebyshev.Chebyshev.fit(s, fn(np.sqrt(s)), terms - 1, domain=[0.0, 0.25])
    return [float(c) for c in fit.convert(kind=np.polynomial.Polynomial, domain=[-1, 1]).coef]


COS_COEF = _poly(lambda t: np.cos(2 * np.pi * t), 8)
SIN_COEF = _poly(lambda t: np.sin(2 * np.pi * t) / t, 7)


def _horner(coef, s):
    out = jnp.full_like(s, coef[-1])
    for c in coef[-2::-1]:
        out = out * s + c
    return out


def _fine(turns, steps):
    t = turns * steps
    t = t - jnp.round(t)
    s = t * t
    return _horner(COS_COEF, s), t * _horner(SIN_COEF, s)


def _powers(turns, steps, scale):
    er, ei = _fine(turns, steps)
    z4r = jnp.broadcast_to(er[4:5], er.shape)
    z4i = jnp.broadcast_to(ei[4:5], ei.shape)

    def square(r, i):
        return r * r - i * i, 2.0 * (r * i)

    z1 = square(z4r, z4i)
    z2 = square(*z1)
    z3 = (z1[0] * z2[0] - z1[1] * z2[1], z1[0] * z2[1] + z1[1] * z2[0])
    z4 = square(*z2)
    if scale is not None:
        wr, wi = scale
        er, ei = er * wr - ei * wi, er * wi + ei * wr
    real = [None] * 8
    imag = [None] * 8
    real[4], imag[4] = er, ei
    for a, (zr, zi) in ((1, z1), (2, z2), (3, z3), (4, z4)):
        rr, ii, ri, ir = er * zr, ei * zi, er * zi, ei * zr
        real[4 - a], imag[4 - a] = rr + ii, ir - ri
        if a < 4:
            real[4 + a], imag[4 + a] = rr - ii, ri + ir
    return jnp.concatenate(real + imag, axis=0).astype(jnp.bfloat16)


def _block_product(block_ref, index, steps):
    left, right = [], []
    for h in range(2):
        def row(k):
            return jnp.broadcast_to(block_ref[index, 2 * k + h : 2 * k + h + 1, :], (8, LANES))

        left.append(_powers(row(2), steps, (row(0), row(1))))
        right.append(_powers(row(3), steps, None))
    return lax.dot_general(
        jnp.concatenate(left, axis=1),
        jnp.concatenate(right, axis=1),
        (((1,), (1,)), ((), ())),
        preferred_element_type=jnp.float32,
    )


def _split(x):
    hi = x.astype(jnp.bfloat16)
    lo = (x - hi.astype(jnp.float32)).astype(jnp.bfloat16)
    return hi, lo


def _combine(four, sign):
    return four[:SG] + pltpu.roll(four[SG:], SG, 1) * sign


def facet_kernel(
    shift,
    subs,
    count_ref,
    keys_ref,
    place_ref,
    vis_ref,
    block_ref,
    screen_a_ref,
    screen_b_ref,
    right_ref,
    left_ref,
    mine_ref,
    theirs_ref,
    sums,
    facet,
    found,
):
    trash = sums.shape[0] - 1
    steps = lax.broadcasted_iota(jnp.int32, (8, LANES), 0).astype(jnp.float32)
    lane = lax.broadcasted_iota(jnp.int32, (SG, LANES), 1)
    sign = jnp.where(lane < SG, -1.0, 1.0)
    facet[...] = jnp.zeros_like(facet)
    count = count_ref[0]

    def grid_blocks(step, carry):
        last_sub, slot = carry
        jobs = []
        for k in range(UNROLL):
            at = step * UNROLL + k
            key = keys_ref[jnp.minimum(at, keys_ref.shape[0] - 1)]
            real = at < count
            index = jnp.where(real, key & ((1 << shift) - 1), 0)
            sub = jnp.where(real, key >> shift, last_sub)
            fresh = sub != last_sub
            slot = slot + fresh.astype(jnp.int32)
            last_sub = sub
            found[jnp.maximum(slot, 0)] = sub
            jobs.append((_block_product(block_ref, index, steps), fresh, jnp.where(real, slot, trash)))
        for product, fresh, where in jobs:
            sums[where] = jnp.where(fresh, 0.0, sums[where]) + product
        return last_sub, slot

    _, top = lax.fori_loop(
        0, (count + UNROLL - 1) // UNROLL, grid_blocks, (jnp.int32(-1), jnp.int32(-1))
    )
    touched = top + 1

    def place_subs(step, carry):
        pieces = []
        for k in range(FFT_UNROLL):
            at = step * FFT_UNROLL + k
            real = at < touched
            at = jnp.minimum(at, touched - 1)
            sub = found[at]
            corner_u, corner_v, plane = place_ref[sub], place_ref[subs + sub], place_ref[2 * subs + sub]
            image = _combine(sums[at], sign)
            masked = image * screen_a_ref[plane] + pltpu.roll(image, SG, 1) * screen_b_ref[plane]
            hi, lo = _split(masked)
            wide = jnp.dot(
                jnp.concatenate([hi, lo], axis=1), right_ref[...], preferred_element_type=jnp.float32
            )
            half = wide[:, :LANES] + wide[:, LANES:]
            hi, lo = _split(half)
            four = jnp.dot(
                left_ref[...],
                jnp.concatenate([hi, lo, hi, jnp.zeros_like(hi)], axis=0),
                preferred_element_type=jnp.float32,
            )
            spectrum = _combine(four, sign)
            off_v = corner_v & (FV - 1)
            pieces.append((spectrum, real, corner_u & (FU - 1), off_v >> 7, off_v & (LANES - 1)))
        for spectrum, real, off_u, tile, s in pieces:
            turned = pltpu.roll(spectrum, s, 1)
            other = pltpu.roll(turned, SG, 1)
            begin = jnp.where(real, s, LANES)
            end = jnp.where(real, s + SG, 0)
            first = (lane >= begin) & (lane < end)
            second = lane < end - LANES
            rows = pl.ds(off_u, SG)
            spots = [(part, tile + t, rows) for part in range(2) for t in range(2)]
            before = [facet[spot] for spot in spots]
            parts = [jnp.where(m, v, 0.0) for v in (turned, other) for m in (first, second)]
            for spot, old, new in zip(spots, before, parts):
                facet[spot] = old + new
        return carry

    lax.fori_loop(0, (touched + FFT_UNROLL - 1) // FFT_UNROLL, place_subs, 0)
    half = TILES // 2
    own = vis_ref[0] * half
    far = (1 - vis_ref[0]) * half
    for part in range(2):
        for t in range(half):
            mine_ref[part, :, t * LANES : (t + 1) * LANES] = facet[part, own + t]
            theirs_ref[part, :, t * LANES : (t + 1) * LANES] = facet[part, far + t]


def gather_kernel(n_col, n_row, chunks, mine_ref, out_ref, ring_send, ring_recv, row_send, row_recv, own_sem):
    col, row = lax.axis_index("col"), lax.axis_index("row")
    right, left = lax.rem(col + 1, n_col), lax.rem(col + n_col - 1, n_col)
    size = mine_ref.shape[0]
    mesh_ids = pl.DeviceIdType.MESH
    barrier = pltpu.get_barrier_semaphore()
    for peer in (left, right):
        pl.semaphore_signal(barrier, inc=1, device_id={"col": peer}, device_id_type=mesh_ids)
    for j in range(1, n_row):
        pl.semaphore_signal(
            barrier, inc=1, device_id={"row": lax.rem(row + j, n_row)}, device_id_type=mesh_ids
        )
    pl.semaphore_wait(barrier, 1 + n_row)

    def slot(back, at_row, k):
        source = lax.rem(col + n_col - back, n_col) * n_row + at_row
        first, count = chunks[k]
        return out_ref.at[pl.ds(source * size + first, count)]

    def from_here(step, at_row, k):
        first, count = chunks[k]
        return mine_ref.at[pl.ds(first, count)] if step == 0 else slot(step, at_row, k)

    def ring(step, j, k):
        at_row = lax.rem(row + j, n_row)
        return pltpu.make_async_remote_copy(
            src_ref=from_here(step, at_row, k) if j == 0 else slot(step, at_row, k),
            dst_ref=slot(step, at_row, k),
            send_sem=ring_send.at[step, j, k],
            recv_sem=ring_recv.at[step, j, k],
            device_id={"col": right},
            device_id_type=mesh_ids,
        )

    def across(step, j, k):
        return pltpu.make_async_remote_copy(
            src_ref=from_here(step, row, k),
            dst_ref=slot(step, row, k),
            send_sem=row_send.at[step, j - 1, k],
            recv_sem=row_recv.at[step, j - 1, k],
            device_id={"row": lax.rem(row + j, n_row)},
            device_id_type=mesh_ids,
        )

    sent = []

    def start(copy):
        copy.start()
        sent.append(copy)

    others = range(1, n_row)
    late = range(1, len(chunks))
    for j in others:
        start(across(0, j, 0))
    for k in range(len(chunks)):
        start(ring(0, 0, k))
    own = pltpu.make_async_copy(
        mine_ref, out_ref.at[pl.ds((col * n_row + row) * size, size)], own_sem
    )
    own.start()
    for k in late:
        for j in others:
            start(across(0, j, k))
    for j in others:
        across(0, n_row - j, 0).wait_recv()
        start(ring(0, j, 0))
    for step in range(1, n_col):
        for k in late:
            ring(step - 1, 0, k).wait_recv()
            if step < n_col - 1:
                start(ring(step, 0, k))
            for j in others:
                start(across(step, j, k))
        for j in range(n_row):
            ring(step - 1, j, 0).wait_recv()
            if step < n_col - 1:
                start(ring(step, j, 0))
    own.wait()
    for copy in sent:
        copy.wait_send()
    for step in range(n_col):
        for k in late:
            for j in others:
                across(step, j, k).wait_recv()


def gather_blocks(payload, n_col, n_row):
    size = payload.shape[0]
    early = size // 6
    ends = [0] + [early + (size - early) * k // 4 for k in range(5)]
    chunks = [(ends[k], ends[k + 1] - ends[k]) for k in range(5)]
    hbm = pl.BlockSpec(memory_space=pl.ANY)
    return pl.pallas_call(
        functools.partial(gather_kernel, n_col, n_row, chunks),
        out_shape=jax.ShapeDtypeStruct((n_col * n_row * size,) + payload.shape[1:], payload.dtype),
        in_specs=[hbm],
        out_specs=hbm,
        scratch_shapes=[
            pltpu.SemaphoreType.DMA((n_col - 1, n_row, 5)),
            pltpu.SemaphoreType.DMA((n_col - 1, n_row, 5)),
            pltpu.SemaphoreType.DMA((n_col, n_row - 1, 5)),
            pltpu.SemaphoreType.DMA((n_col, n_row - 1, 5)),
            pltpu.SemaphoreType.DMA,
        ],
        compiler_params=pltpu.CompilerParams(collective_id=0, has_side_effects=True),
        name="gather",
    )(payload)


def dft_tables():
    k = np.arange(SG)
    angle = 2.0 * np.pi * (np.outer(k, k) % SG) / SG
    re, im = np.cos(angle), -np.sin(angle)
    right = np.block([[re, im], [-im, re]]) / (SG * math.sqrt(BV))
    left = np.concatenate([re, im], axis=0)

    def split(x):
        hi = np.asarray(x, jnp.bfloat16).astype(np.float64)
        return hi, x - hi

    rhi, rlo = split(right)
    lhi, llo = split(left)
    right = np.block([[rhi, rlo], [rhi, np.zeros_like(rlo)]])
    left = np.concatenate([lhi, lhi, llo, np.zeros_like(llo)], axis=1)
    return jnp.asarray(right, jnp.bfloat16), jnp.asarray(left, jnp.bfloat16)


def on_device(
    visibilities,
    coords,
    block_subgrid,
    baseline_ids,
    live_blocks,
    subgrid_place,
    baseline_weight,
    tapering,
    plane_phase,
):
    nblocks = visibilities.shape[0]
    n_col = lax.axis_size("col")
    n_row = lax.axis_size("row")
    n_vis = lax.axis_size("vis")
    devices = n_col * n_row * n_vis
    facets = n_col * n_row
    sub_dev = subgrid_place.shape[1]
    subs = devices * sub_dev
    held = facets * nblocks
    max_subs = min(devices * (2 * sub_dev // facets), held)
    vis = lax.axis_index("vis")
    live = jnp.arange(nblocks) < live_blocks[0]

    swap = [(d, n_vis - 1 - d) for d in range(n_vis)]
    label = jnp.where(live, block_subgrid, -1)
    meta = jnp.concatenate([label, subgrid_place.reshape(-1)]).astype(jnp.float32)
    meta = jnp.pad(meta, (0, 8 * LANES - meta.shape[0])).reshape(1, 8, LANES)
    other = lax.ppermute(meta, "vis", swap)
    pair = jnp.where(vis == 0, jnp.concatenate([meta, other]), jnp.concatenate([other, meta]))

    weight = jnp.where(live, baseline_weight.at[baseline_ids].get(mode="promise_in_bounds"), 0.0)
    weighted = visibilities.astype(jnp.float32) * weight[:, None, None]
    payload = jnp.concatenate([weighted, coords], axis=1).reshape(nblocks, 8, LANES)
    stride = nblocks + n_vis
    blocks = gather_blocks(jnp.concatenate([payload, pair]), n_col, n_row)

    meta = blocks.reshape(facets, stride, 8, LANES)[:, nblocks:].astype(jnp.int32)
    meta = meta.reshape(facets, n_vis, 8 * LANES)
    labels = lax.dynamic_index_in_dim(meta, vis, axis=1, keepdims=False)[:, :nblocks]
    labels = labels.reshape(held)
    place = meta.reshape(devices, -1)[:, nblocks : nblocks + 3 * sub_dev].reshape(devices, 3, sub_dev)
    here = (place[:, 0] // FU == lax.axis_index("col")) & (place[:, 1] // FV == lax.axis_index("row"))
    place = place.transpose(1, 0, 2)
    owner = (labels[:, None] // sub_dev == jnp.arange(devices)).astype(jnp.float32)
    local = labels[:, None] % sub_dev == jnp.arange(sub_dev)
    named = jnp.dot(owner, here.astype(jnp.float32))
    wanted = (labels >= 0) & (jnp.sum(jnp.where(local, named, 0.0), axis=1) > 0.5)
    index = jnp.arange(facets)[:, None] * stride + jnp.arange(nblocks)[None, :]
    index = index.reshape(held).astype(jnp.int32)
    shift = max(1, (facets * stride - 1).bit_length())
    keys = jnp.where(wanted, (labels << shift) + index, BIG)
    keys = lax.sort(keys, is_stable=False)
    count = jnp.sum(wanted.astype(jnp.int32)).reshape(1)

    screen_re = tapering * jnp.cos(plane_phase)
    screen_im = tapering * jnp.sin(plane_phase)
    screen_a = jnp.concatenate([screen_re, screen_re], axis=2)
    screen_b = jnp.concatenate([-screen_im, screen_im], axis=2)
    right, left = dft_tables()

    smem = pl.BlockSpec(memory_space=pltpu.SMEM)
    vmem = pl.BlockSpec(memory_space=pltpu.VMEM)
    half_shape = jax.ShapeDtypeStruct((2, FU, FV // n_vis), jnp.float32)
    mine, theirs = pl.pallas_call(
        functools.partial(facet_kernel, shift, subs),
        out_shape=(half_shape, half_shape),
        in_specs=[smem] * 4 + [vmem] * 5,
        out_specs=(vmem, vmem),
        scratch_shapes=[
            pltpu.VMEM((max_subs + 1, 2 * SG, 2 * SG), jnp.float32),
            pltpu.VMEM((2, TILES + 1, FU, LANES), jnp.float32),
            pltpu.SMEM((max_subs + 8,), jnp.int32),
        ],
        compiler_params=pltpu.CompilerParams(vmem_limit_bytes=56 * 1024 * 1024),
        name="facet",
    )(count, keys, place.reshape(-1), vis.reshape(1), blocks, screen_a, screen_b, right, left)
    return mine + lax.ppermute(theirs, "vis", swap)


def solution(mesh):
    spread = ("band", "col", "row", "vis")
    in_specs = (
        P(spread, None, None),
        P(spread, None, None),
        P(spread),
        P(spread),
        P(spread),
        P(None, spread),
        P(),
        P(),
        P(),
    )
    out_specs = P(None, ("band", "col"), ("row", "vis"))
    return jax.shard_map(
        on_device, mesh=mesh, in_specs=in_specs, out_specs=out_specs, check_vma=False
    )
```
